256 devices in a mesh: dp: 256 (over x, y, z, core).
Axes of the slice: x: 4, y: 4, z: 8, core: 2. Of those that a mesh axis runs over, the one named last changes fastest.
Arguments:
- images: bfloat16 [262144, 1152], P('dp'), may hold values from -0.1875 to 0.1875
- texts: bfloat16 [262144, 1152], P('dp'), may hold values from -0.1875 to 0.1875
- positive: int32 [262144], P('dp'), may hold values from 0 to 262143, as said below
- loss_cotangent: float32 [], replicated, may hold values from 256 to 1024
Outputs:
- image_grad: bfloat16 [262144, 1152], P('dp')
- text_grad: float32 [262144, 1152], P('dp')
The draws below stay inside these ranges and needn't reach their ends.
Inputs may be any that keep to these rules, and one draw needn't show every extreme that they name: `positive`: the 1024 rows of each block name every text row of that same block exactly once.
All inputs are finite; a program needn't handle non-finite values.
Results may differ from the reference program's by a relative error of at most 0.005.
Values may be sent and summed in bfloat16 or wider, within the bound.
No kernel may reach another device: no remote copies, remote signals or barrier semaphores. Data moves between devices by JAX's collectives and lax.ppermute only.
A program may use at most 64 MiB of HBM per device.

```python
import math
import jax
import jax.numpy as jnp
from jax import lax

D = 1152
TOKENS_PER_UNIT = 1024
BLOCKS = 256
TOKENS = 262144


def draw_positive(key, part):
    key = jax.random.fold_in(key, 1)
    block_keys = jax.random.split(key, BLOCKS)
    orders = jax.vmap(lambda sub_key: jax.random.permutation(sub_key, TOKENS_PER_UNIT))(block_keys)
    starts = (jnp.arange(BLOCKS, dtype=jnp.int32) * TOKENS_PER_UNIT)[:, None]
    return (orders.astype(jnp.int32) + starts).reshape(-1).astype(jnp.int32)


def shard_levels(own_key, dims, shards, least, high):
    factor_of, own = 1.0, jax.random.fold_in(own_key, 6)
    for axis_at, parts in shards:
        steps = jnp.exp(jax.random.uniform(jax.random.fold_in(own, axis_at), (parts,), jnp.float32, least / len(shards), high / len(shards)))
        factor_of = factor_of * jnp.repeat(steps, dims[axis_at] // parts).reshape([-1 if axis == axis_at else 1 for axis in range(len(dims))])
    return factor_of


def gaussian(stream_key, extent, spread, most, pieces=(), kind=jnp.bfloat16):
    gain = shard_levels(stream_key, extent, pieces, -0.22, 0.18) if pieces else 1.0
    entries = jax.random.normal(stream_key, extent, jnp.float32) * spread * gain
    return jnp.minimum(jnp.maximum(entries, -most), most).astype(kind)


def setup_inputs(seed: int = 0) -> dict:
    key_list = jax.random.split(jax.random.key(seed), 5)
    return {
        "images": gaussian(key_list[0], (TOKENS, D), D ** -0.5, 0.1875, ((0, 256),)),
        "texts": gaussian(key_list[1], (TOKENS, D), D ** -0.5, 0.1875, ((0, 256),)),
        "positive": draw_positive(jax.random.fold_in(key_list[4], 71), 0),
        "loss_cotangent": jnp.clip(jnp.exp(jax.random.uniform(key_list[3], (), jnp.float32, math.log(256.0), math.log(1024.0))), 256.0, 1024.0),
    }


LOGIT_SCALE = 10.0
SCORE_OFFSET = -2.0


def tile_terms(packed):
    image_tile_rows, text_tile_rows, earlier_block, match_block, block_id = packed
    columns = jnp.arange(TOKENS_PER_UNIT, dtype=jnp.int32)
    local_match = match_block - block_id * TOKENS_PER_UNIT
    labels = (local_match[:, None] == columns[None, :]).astype(jnp.float32)
    pair_scores = LOGIT_SCALE * jnp.dot(image_tile_rows, text_tile_rows.T, preferred_element_type=jnp.float32) + SCORE_OFFSET
    remote_texts = LOGIT_SCALE * jnp.dot(image_tile_rows, earlier_block.T, preferred_element_type=jnp.float32) + SCORE_OFFSET
    own_coef = (jax.nn.sigmoid(pair_scores) - labels).astype(jnp.bfloat16)
    far_coef = jax.nn.sigmoid(remote_texts).astype(jnp.bfloat16)
    image_part = jnp.dot(own_coef, text_tile_rows, preferred_element_type=jnp.float32) + jnp.dot(far_coef, earlier_block, preferred_element_type=jnp.float32)
    own_text = jnp.dot(own_coef.T, image_tile_rows, preferred_element_type=jnp.float32)
    far_text = jnp.dot(far_coef.T, image_tile_rows, preferred_element_type=jnp.float32)
    return image_part, own_text, far_text


def reference(images, texts, positive, loss_cotangent):
    image_blocks = images.reshape(BLOCKS, TOKENS_PER_UNIT, D)
    text_blocks = texts.reshape(BLOCKS, TOKENS_PER_UNIT, D)
    prior_blocks = jnp.roll(text_blocks, 1, axis=0)
    match_blocks = positive.reshape(BLOCKS, TOKENS_PER_UNIT)
    block_ids = jnp.arange(BLOCKS, dtype=jnp.int32)
    image_part, own_text, far_text = lax.map(tile_terms, (image_blocks, text_blocks, prior_blocks, match_blocks, block_ids))
    scale_factor = loss_cotangent * (LOGIT_SCALE / TOKENS_PER_UNIT)
    image_grad = (scale_factor * image_part).astype(jnp.bfloat16).reshape(TOKENS, D)
    text_grad = (scale_factor * own_text + scale_factor * jnp.roll(far_text, -1, axis=0)).reshape(TOKENS, D)
    return image_grad, text_grad
```

```python
import functools
import math

import jax
import jax.numpy as jnp
from jax import lax
from jax.experimental import pallas as pl
from jax.experimental.pallas import tpu as pltpu
from jax.sharding import PartitionSpec as P

LOGIT_SCALE = 10.0
SCORE_OFFSET = -2.0
FAR_ROWS = (768, 256)
NEAR_ROWS = (512, 512)
OWN_TILE = 256
PICK_TILE = 128
PAIR_TILE = 512
NT = (((1,), (1,)), ((), ()))
NN = (((1,), (0,)), ((), ()))
TN = (((0,), (0,)), ((), ()))
VMEM = pl.BlockSpec(memory_space=pltpu.VMEM)
SMEM = pl.BlockSpec(memory_space=pltpu.SMEM)
ANY = pl.BlockSpec(memory_space=pl.ANY)


def mm(a, b, dims):
    return lax.dot_general(a, b, dims, preferred_element_type=jnp.float32)


def sigmoid(product):
    per_bit = 1.0 / math.log(2.0)
    return 1.0 / (1.0 + jnp.exp2(product * (-LOGIT_SCALE * per_bit) - SCORE_OFFSET * per_bit))


def in_vmem(x):
    return pltpu.with_memory_space_constraint(x, pltpu.VMEM)


def in_hbm(x):
    return pltpu.with_memory_space_constraint(x, pltpu.HBM)


def params(mib):
    return pltpu.CompilerParams(vmem_limit_bytes=mib << 20)


def cost(matmuls, rows, cols, depth):
    return pl.CostEstimate(flops=2 * matmuls * rows * cols * depth, bytes_accessed=0, transcendentals=0)


def is_even():
    return lax.rem(lax.axis_index("dp"), 2) == 0


def pick_kernel(starts, scaled, images_ref, texts_ref, *refs):
    n = len(starts)
    outs, sems = refs[-n - 1 : -1], refs[-1]
    if scaled:
        cotangent_ref, scale_ref = refs[0], refs[-n - 2]
    even = is_even()

    def copies(i, source):
        start, total = starts[i][0], outs[i].shape[0]
        return [
            pltpu.make_async_copy(
                source.at[pl.ds(start + at, PICK_TILE), :], outs[i].at[pl.ds(at, PICK_TILE), :], sems.at[i, at // PICK_TILE]
            )
            for at in range(0, total, PICK_TILE)
        ]

    def begin(flipped):
        for i, (_, flip) in enumerate(starts):
            for copy in copies(i, images_ref if flip == flipped else texts_ref):
                copy.start()

    @pl.when(even)
    def _():
        begin(False)

    @pl.when(jnp.logical_not(even))
    def _():
        begin(True)

    for i in range(n):
        for copy in copies(i, images_ref):
            copy.wait()
    if scaled:
        total = images_ref.shape[0]
        scale_ref[...] = jnp.full(scale_ref.shape, cotangent_ref[0] * (LOGIT_SCALE / total), jnp.float32)


def pick(images, texts, wanted, cotangent=None, after=()):
    depth = images.shape[1]
    n = len(wanted)
    scale = () if cotangent is None else (pltpu.VMEM((8, depth), jnp.float32),)
    return pl.pallas_call(
        functools.partial(pick_kernel, [(w[0], w[2]) for w in wanted], bool(scale)),
        out_shape=scale + tuple(pltpu.VMEM((w[1], depth), images.dtype) for w in wanted),
        in_specs=[ANY] * 2 + [SMEM] * len(scale) + [ANY] * len(after),
        out_specs=(VMEM,) * (n + len(scale)),
        scratch_shapes=[pltpu.SemaphoreType.DMA((n, max(w[1] for w in wanted) // PICK_TILE))],
        compiler_params=params(6),
        cost_estimate=pl.CostEstimate(flops=0, bytes_accessed=4 * depth * sum(w[1] for w in wanted), transcendentals=0),
    )(in_hbm(images), in_hbm(texts), *([] if cotangent is None else [cotangent]), *after)


def across(coef, others):
    total, at = None, 0
    for other in others:
        part = mm(coef[:, at : at + other.shape[0]], other, NN)
        total = part if total is None else total + part
        at += other.shape[0]
    return total


def own_kernel(chunks, match_ref, *refs):
    a_refs, b_refs, (acc_a, acc_b) = refs[:chunks], refs[chunks:-2], refs[-2:]
    rows = acc_b.shape[0]
    even = is_even()
    first = lax.axis_index("dp") * rows
    match_row = match_ref[...] - first
    others = [ref[...] for ref in b_refs]
    tiles = [(ref, start) for ref in a_refs for start in range(0, ref.shape[0], OWN_TILE)]

    def load(t):
        ref, start = tiles[t]
        return ref[start : start + OWN_TILE, :]

    def product_of(t):
        return jnp.concatenate([mm(load(t), other, NT) for other in others], axis=1)

    product = product_of(0)
    for t in range(len(tiles)):
        at = t * OWN_TILE
        if t + 1 < len(tiles):
            following = product_of(t + 1)
        match_tile = jnp.broadcast_to(match_ref[:, at : at + OWN_TILE] - first, (128, OWN_TILE)).T
        match_col = jnp.concatenate([match_tile] * (rows // 128), axis=1)
        lane = lax.broadcasted_iota(jnp.int32, (OWN_TILE, rows), 1)
        row = lax.broadcasted_iota(jnp.int32, (OWN_TILE, rows), 0) + at
        gap = jnp.where(even, match_col - lane, match_row - row)
        coef = (sigmoid(product) - jnp.where(gap == 0, 1.0, 0.0)).astype(jnp.bfloat16)
        acc_a[at : at + OWN_TILE, :] = across(coef, others)
        term = mm(coef, load(t), TN)
        if t == 0:
            acc_b[...] = term
        else:
            acc_b[...] += term
        product = following

def own_tile(own, base, match):
    rows, depth = sum(o.shape[0] for o in base), base[0].shape[1]
    n = len(own)
    return pl.pallas_call(
        functools.partial(own_kernel, n),
        out_shape=(
            pltpu.VMEM((rows, depth), jnp.float32),
            pltpu.VMEM((rows, depth), jnp.float32),
        ),
        in_specs=[VMEM] * (n + 1 + len(base)),
        out_specs=(VMEM, VMEM),
        compiler_params=params(20),
        cost_estimate=cost(3, rows, rows, depth),
    )(in_vmem(match), *[in_vmem(o) for o in own], *[in_vmem(o) for o in base])


def pair_tiles(own_refs, other_refs, tile):
    tiles = [(ref, start) for ref in own_refs for start in range(0, ref.shape[0], tile)]
    sizes = [min(tile, ref.shape[0] - start) for ref, start in tiles]
    others = [ref[...] for ref in other_refs]

    def products(t):
        ref, start = tiles[t]
        own = ref[start : start + sizes[t], :]
        return [mm(own, other, NT) for other in others]

    at, held = 0, products(0)
    for t in range(len(tiles)):
        following = products(t + 1) if t + 1 < len(tiles) else None
        term = None
        for product, other in zip(held, others, strict=True):
            part = mm(sigmoid(product).astype(jnp.bfloat16), other, NN)
            term = part if term is None else term + part
        yield t, at, sizes[t], term
        at += sizes[t]
        held = following


def last_kernel(chunks, parts, to_image, tile, *refs):
    own_refs, other_refs, rest = refs[:chunks], refs[chunks : chunks + parts], refs[chunks + parts :]
    acc_ref, scale_ref = rest[:2]
    image_ref, text_ref, wide, narrow, sems = rest[-5:]
    even = is_even()

    def go(stage, out_ref):
        scale = scale_ref[0:1, :]
        copies = []
        for t, at, size, term in pair_tiles(own_refs, other_refs, tile):
            rows = pl.ds(at, size)
            stage[rows, :] = (scale * (acc_ref[rows, :] + term)).astype(stage.dtype)
            copies.append(pltpu.make_async_copy(stage.at[rows, :], out_ref.at[rows, :], sems.at[t]))
            copies[-1].start()
        for copy in copies:
            copy.wait()

    @pl.when(even == to_image)
    def _():
        go(narrow, image_ref)

    @pl.when(even != to_image)
    def _():
        go(wide, text_ref)


def last(own, other, acc, scale, outs, to_image):
    rows, depth = acc.shape
    given = [] if outs is None else list(outs)
    n, parts = len(own), len(other)
    return pl.pallas_call(
        functools.partial(last_kernel, n, parts, to_image, PAIR_TILE),
        out_shape=(
            jax.ShapeDtypeStruct((rows, depth), jnp.bfloat16),
            jax.ShapeDtypeStruct((rows, depth), jnp.float32),
        ),
        in_specs=[VMEM] * (n + parts + 2) + [ANY] * len(given),
        out_specs=(ANY, ANY),
        scratch_shapes=[
            pltpu.VMEM((rows, depth), jnp.float32),
            pltpu.VMEM((rows, depth), jnp.bfloat16),
            pltpu.SemaphoreType.DMA((8,)),
        ],
        input_output_aliases={n + parts + 2 + i: i for i in range(len(given))},
        compiler_params=params(20),
        cost_estimate=cost(2, rows, sum(o.shape[0] for o in other), depth),
    )(*[in_vmem(o) for o in own], *[in_vmem(o) for o in other], in_vmem(acc), in_vmem(scale), *given)


def middle_kernel(chunks, *refs):
    own_refs, other_ref, acc_ref, out_ref = refs[:chunks], refs[chunks], refs[chunks + 1], refs[-1]
    for _, at, size, term in pair_tiles(own_refs, [other_ref], PAIR_TILE):
        rows = pl.ds(at, size)
        out_ref[rows, :] = acc_ref[rows, :] + term


def middle(own, other, acc, after):
    rows, depth = acc.shape
    n = len(own)
    return pl.pallas_call(
        functools.partial(middle_kernel, n),
        out_shape=pltpu.VMEM((rows, depth), jnp.float32),
        in_specs=[VMEM] * (n + 2) + [ANY] * len(after),
        out_specs=VMEM,
        input_output_aliases={n + 1: 0},
        compiler_params=params(16),
        cost_estimate=cost(2, rows, other.shape[0], depth),
    )(*[in_vmem(o) for o in own], in_vmem(other), in_vmem(acc), *[in_hbm(o) for o in after])


def spans(counts, flip):
    start = 0
    for count in counts:
        yield start, count, flip
        start += count


def local(images, texts, positive, loss_cotangent):
    rows = images.shape[0]
    size = lax.axis_size("dp")
    far_pairs = [(p, (p - 1) % size if p % 2 == 0 else (p + 1) % size) for p in range(size)]
    near_pairs = [(p, p + 1 if p % 2 == 0 else p - 1) for p in range(size)]
    (first,) = pick(images, texts, [(0, FAR_ROWS[0], False)])
    wanted = list(spans(FAR_ROWS, False))[1:] + list(spans(NEAR_ROWS, True))
    cotangent, first = lax.optimization_barrier((loss_cotangent, first))
    scale, *picked = pick(images, texts, wanted, cotangent.reshape(1), (first,))
    far_own, near_own = [first, *picked[: len(FAR_ROWS) - 1]], picked[len(FAR_ROWS) - 1 :]
    far = [lax.ppermute(part, "dp", far_pairs) for part in far_own]
    near = [lax.ppermute(part, "dp", near_pairs) for part in near_own]
    far_acc, near_acc = own_tile(far_own, near_own, positive.reshape(1, rows))
    outs = last(near_own, near, near_acc, scale, None, False)
    for part in far[:-1]:
        far_acc = middle(far_own, part, far_acc, outs)
    return last(far_own, far[-1:], far_acc, scale, outs, True)


def solution(mesh):
    in_specs = (P("dp", None), P("dp", None), P("dp"), P())
    out_specs = (P("dp", None), P("dp", None))
    return jax.shard_map(local, mesh=mesh, in_specs=in_specs, out_specs=out_specs, check_vma=False)
```

```python
import functools
import math

import jax
import jax.numpy as jnp
from jax import lax
from jax.experimental import pallas as pl
from jax.experimental.pallas import tpu as pltpu
from jax.sharding import PartitionSpec as P

LOGIT_SCALE = 10.0
SCORE_OFFSET = -2.0
FAR_ROWS = (768, 256)
NEAR_ROWS = (512, 512)
OWN_TILE = 256
HEAD_TILES = 2
LAST_TILE = 256
PICK_TILE = 128
PAIR_TILE = 512
NT = (((1,), (1,)), ((), ()))
NN = (((1,), (0,)), ((), ()))
TN = (((0,), (0,)), ((), ()))
VMEM = pl.BlockSpec(memory_space=pltpu.VMEM)
SMEM = pl.BlockSpec(memory_space=pltpu.SMEM)
ANY = pl.BlockSpec(memory_space=pl.ANY)


def mm(a, b, dims):
    return lax.dot_general(a, b, dims, preferred_element_type=jnp.float32)


def sigmoid(product):
    per_bit = 1.0 / math.log(2.0)
    return 1.0 / (1.0 + jnp.exp2(product * (-LOGIT_SCALE * per_bit) - SCORE_OFFSET * per_bit))


def in_vmem(x):
    return pltpu.with_memory_space_constraint(x, pltpu.VMEM)


def in_hbm(x):
    return pltpu.with_memory_space_constraint(x, pltpu.HBM)


def params(mib):
    return pltpu.CompilerParams(vmem_limit_bytes=mib << 20)


def cost(matmuls, rows, cols, depth):
    return pl.CostEstimate(flops=2 * matmuls * rows * cols * depth, bytes_accessed=0, transcendentals=0)


def is_even():
    return lax.rem(lax.axis_index("dp"), 2) == 0


def fetches(starts, images_ref, texts_ref, outs, sems):
    even = is_even()

    def copies(i, source):
        return [
            pltpu.make_async_copy(
                source.at[pl.ds(starts[i][0] + at, PICK_TILE), :], outs[i].at[pl.ds(at, PICK_TILE), :], sems.at[i, at // PICK_TILE]
            )
            for at in range(0, outs[i].shape[0], PICK_TILE)
        ]

    def begin(flipped):
        for i, (_, _, flip) in enumerate(starts):
            for copy in copies(i, images_ref if flip == flipped else texts_ref):
                copy.start()

    @pl.when(even)
    def _():
        begin(False)

    @pl.when(jnp.logical_not(even))
    def _():
        begin(True)

    def wait(i):
        for copy in copies(i, images_ref):
            copy.wait()

    return [functools.partial(wait, i) for i in range(len(starts))]


def semaphores(wanted):
    return pltpu.SemaphoreType.DMA((len(wanted), max(w[1] for w in wanted) // PICK_TILE))


def pick_kernel(wanted, images_ref, texts_ref, *refs):
    for wait in fetches(wanted, images_ref, texts_ref, refs[:-1], refs[-1]):
        wait()


def pick(images, texts, wanted):
    depth = images.shape[1]
    return pl.pallas_call(
        functools.partial(pick_kernel, wanted),
        out_shape=tuple(pltpu.VMEM((w[1], depth), images.dtype) for w in wanted),
        in_specs=[ANY] * 2,
        out_specs=(VMEM,) * len(wanted),
        scratch_shapes=[semaphores(wanted)],
        compiler_params=params(1),
    )(in_hbm(images), in_hbm(texts))


def across(coef, others):
    total, at = None, 0
    for other in others:
        part = mm(coef[:, at : at + other.shape[0]], other, NN)
        total = part if total is None else total + part
        at += other.shape[0]
    return total


def own_tiles(tiles, at, other_refs, match_ref, acc_a, acc_b):
    rows = acc_b.shape[0]
    even = is_even()
    first = lax.axis_index("dp") * rows
    match_row = match_ref[...] - first

    def load(t):
        ref, start = tiles[t]
        return ref[start : start + OWN_TILE, :]

    others = [ref[...] for ref in other_refs]

    def product_of(t):
        return jnp.concatenate([mm(load(t), other, NT) for other in others], axis=1)

    product = product_of(0)
    for t in range(len(tiles)):
        following = product_of(t + 1) if t + 1 < len(tiles) else None
        match_tile = jnp.broadcast_to(match_ref[:, at : at + OWN_TILE] - first, (128, OWN_TILE)).T
        match_col = jnp.concatenate([match_tile] * (rows // 128), axis=1)
        lane = lax.broadcasted_iota(jnp.int32, (OWN_TILE, rows), 1)
        row = lax.broadcasted_iota(jnp.int32, (OWN_TILE, rows), 0) + at
        gap = jnp.where(even, match_col - lane, match_row - row)
        coef = (sigmoid(product) - jnp.where(gap == 0, 1.0, 0.0)).astype(jnp.bfloat16)
        acc_a[at : at + OWN_TILE, :] = across(coef, others)
        term = mm(coef, load(t), TN)
        if at == 0:
            acc_b[...] = term
        else:
            acc_b[...] += term
        product = following
        at += OWN_TILE


def tiles_of(refs):
    return [(ref, start) for ref in refs for start in range(0, ref.shape[0], OWN_TILE)]


def head_kernel(wanted, bases, images_ref, texts_ref, match_ref, cotangent_ref, first_ref, *refs):
    *outs, acc_a, acc_b, scale_ref, sems = refs
    waits = fetches(wanted, images_ref, texts_ref, outs, sems)
    scale_ref[...] = jnp.full(scale_ref.shape, cotangent_ref[0] * (LOGIT_SCALE / acc_b.shape[0]), jnp.float32)
    tiles = tiles_of([first_ref])[:HEAD_TILES]
    for wait in waits[:bases]:
        wait()
    own_tiles(tiles, 0, outs[:bases], match_ref, acc_a, acc_b)
    for wait in waits[bases:]:
        wait()


def own_head(images, texts, match, cotangent, first, wanted, bases):
    rows, depth = images.shape
    return pl.pallas_call(
        functools.partial(head_kernel, wanted, bases),
        out_shape=(
            *(pltpu.VMEM((w[1], depth), images.dtype) for w in wanted),
            pltpu.VMEM((rows, depth), jnp.float32),
            pltpu.VMEM((rows, depth), jnp.float32),
            pltpu.VMEM((8, depth), jnp.float32),
        ),
        in_specs=[ANY, ANY, VMEM, SMEM, VMEM],
        out_specs=(VMEM,) * (len(wanted) + 3),
        scratch_shapes=[semaphores(wanted)],
        compiler_params=params(16),
        cost_estimate=cost(3, OWN_TILE * HEAD_TILES, rows, depth),
    )(in_hbm(images), in_hbm(texts), in_vmem(match), cotangent, in_vmem(first))


def rest_kernel(chunks, match_ref, *refs):
    a_refs, b_refs, (acc_a, acc_b) = refs[:chunks], refs[chunks:-4], refs[-2:]
    tiles = tiles_of(a_refs)[HEAD_TILES:]
    own_tiles(tiles, HEAD_TILES * OWN_TILE, b_refs, match_ref, acc_a, acc_b)


def own_rest(own, base, match, acc_a, acc_b):
    rows, depth = acc_a.shape
    n, given = len(own), 1 + len(own) + len(base)
    return pl.pallas_call(
        functools.partial(rest_kernel, n),
        out_shape=(pltpu.VMEM((rows, depth), jnp.float32), pltpu.VMEM((rows, depth), jnp.float32)),
        in_specs=[VMEM] * (given + 2),
        out_specs=(VMEM, VMEM),
        input_output_aliases={given: 0, given + 1: 1},
        compiler_params=params(16),
        cost_estimate=cost(3, rows - OWN_TILE * HEAD_TILES, rows, depth),
    )(in_vmem(match), *[in_vmem(o) for o in (*own, *base, acc_a, acc_b)])


def pair_tiles(own_refs, other_refs, tile):
    tiles = [(ref, start) for ref in own_refs for start in range(0, ref.shape[0], tile)]
    sizes = [min(tile, ref.shape[0] - start) for ref, start in tiles]
    others = [ref[...] for ref in other_refs]

    def products(t):
        ref, start = tiles[t]
        own = ref[start : start + sizes[t], :]
        return [mm(own, other, NT) for other in others]

    at, held = 0, products(0)
    for t in range(len(tiles)):
        following = products(t + 1) if t + 1 < len(tiles) else None
        term = None
        for product, other in zip(held, others, strict=True):
            part = mm(sigmoid(product).astype(jnp.bfloat16), other, NN)
            term = part if term is None else term + part
        yield t, at, sizes[t], term
        at += sizes[t]
        held = following


def near_kernel(chunks, *refs):
    own_refs, other_refs, rest = refs[:chunks], refs[chunks : 2 * chunks], refs[2 * chunks :]
    acc_ref, scale_ref, wide_ref, narrow_ref = rest

    def go(out_ref):
        scale = scale_ref[0:1, :]
        for _, at, size, term in pair_tiles(own_refs, other_refs, PAIR_TILE):
            rows = pl.ds(at, size)
            out_ref[rows, :] = (scale * (acc_ref[rows, :] + term)).astype(out_ref.dtype)

    @pl.when(is_even())
    def _():
        go(wide_ref)

    @pl.when(jnp.logical_not(is_even()))
    def _():
        go(narrow_ref)


def near_pair(own, other, acc, scale):
    rows, depth = acc.shape
    n = len(own)
    return pl.pallas_call(
        functools.partial(near_kernel, n),
        out_shape=(pltpu.VMEM((rows, depth), jnp.float32), pltpu.VMEM((rows, depth), jnp.bfloat16)),
        in_specs=[VMEM] * (2 * n + 2),
        out_specs=(VMEM, VMEM),
        input_output_aliases={2 * n: 0},
        compiler_params=params(16),
        cost_estimate=cost(2, rows, rows, depth),
    )(*[in_vmem(o) for o in (*own, *other, acc, scale)])


def last_kernel(chunks, tile, *refs):
    own_refs, other_ref, acc_ref, scale_ref = refs[:chunks], *refs[chunks : chunks + 3]
    image_ref, text_ref, wide, narrow, sems = refs[-5:]

    def go(stage, out_ref):
        scale = scale_ref[0:1, :]
        copies = []
        for t, at, size, term in pair_tiles(own_refs, [other_ref], tile):
            rows = pl.ds(at, size)
            stage[rows, :] = (scale * (acc_ref[rows, :] + term)).astype(stage.dtype)
            copies.append(pltpu.make_async_copy(stage.at[rows, :], out_ref.at[rows, :], sems.at[t]))
            copies[-1].start()
        for copy in copies:
            copy.wait()

    @pl.when(is_even())
    def _():
        go(narrow, image_ref)

    @pl.when(jnp.logical_not(is_even()))
    def _():
        go(wide, text_ref)


def last(own, other, acc, scale, outs, tile):
    rows, depth = acc.shape
    n = len(own)
    return pl.pallas_call(
        functools.partial(last_kernel, n, tile),
        out_shape=(
            jax.ShapeDtypeStruct((rows, depth), jnp.bfloat16),
            jax.ShapeDtypeStruct((rows, depth), jnp.float32),
        ),
        in_specs=[VMEM] * (n + 3) + [ANY] * 2,
        out_specs=(ANY, ANY),
        scratch_shapes=[
            pltpu.VMEM((rows, depth), jnp.float32),
            pltpu.VMEM((rows, depth), jnp.bfloat16),
            pltpu.SemaphoreType.DMA((rows // tile,)),
        ],
        input_output_aliases={n + 3 + i: i for i in range(2)},
        compiler_params=params(16),
        cost_estimate=cost(2, rows, other.shape[0], depth),
    )(*[in_vmem(o) for o in (*own, other, acc, scale)], *outs)


def middle_kernel(chunks, parts, *refs):
    own_refs, other_refs, rest = refs[:chunks], refs[chunks : chunks + parts], refs[chunks + parts :]
    acc_ref, wide_ref, narrow_ref, out_ref, image_ref, text_ref, sems = rest
    tile = acc_ref.shape[0] // sems.shape[0]

    def move(source, target, act):
        for i in range(sems.shape[0]):
            rows = pl.ds(i * tile, tile)
            act(pltpu.make_async_copy(source.at[rows, :], target.at[rows, :], sems.at[i]))

    def moves(act):
        @pl.when(is_even())
        def _():
            move(wide_ref, text_ref, act)

        @pl.when(jnp.logical_not(is_even()))
        def _():
            move(narrow_ref, image_ref, act)

    moves(lambda copy: copy.start())
    for _, at, size, term in pair_tiles(own_refs, other_refs, PAIR_TILE):
        rows = pl.ds(at, size)
        out_ref[rows, :] = acc_ref[rows, :] + term
    moves(lambda copy: copy.wait())


def middle(own, other, acc, done):
    rows, depth = acc.shape
    n, parts = len(own), len(other)
    return pl.pallas_call(
        functools.partial(middle_kernel, n, parts),
        out_shape=(
            pltpu.VMEM((rows, depth), jnp.float32),
            jax.ShapeDtypeStruct((rows, depth), jnp.bfloat16),
            jax.ShapeDtypeStruct((rows, depth), jnp.float32),
        ),
        in_specs=[VMEM] * (n + parts + 3),
        out_specs=(VMEM, ANY, ANY),
        scratch_shapes=[pltpu.SemaphoreType.DMA((4,))],
        input_output_aliases={n + parts: 0},
        compiler_params=params(16),
        cost_estimate=cost(2, rows, sum(o.shape[0] for o in other), depth),
    )(*[in_vmem(o) for o in (*own, *other, acc, *done)])


def spans(counts, flip):
    start = 0
    for count in counts:
        yield start, count, flip
        start += count


def local(images, texts, positive, loss_cotangent):
    rows = images.shape[0]
    size = lax.axis_size("dp")
    far_pairs = [(p, (p - 1) % size if p % 2 == 0 else (p + 1) % size) for p in range(size)]
    near_pairs = [(p, p + 1 if p % 2 == 0 else p - 1) for p in range(size)]
    match = positive.reshape(1, rows)
    (first,) = pick(images, texts, list(spans(FAR_ROWS, False))[:1])
    wanted = list(spans(NEAR_ROWS, True)) + list(spans(FAR_ROWS, False))[1:]
    bases = len(NEAR_ROWS)
    cotangent, first = lax.optimization_barrier((loss_cotangent, first))
    *picked, far_acc, near_acc, scale = own_head(images, texts, match, cotangent.reshape(1), first, wanted, bases)
    near_own, far_own = picked[:bases], [first, *picked[bases:]]
    far = [lax.ppermute(part, "dp", far_pairs) for part in far_own]
    near = [lax.ppermute(part, "dp", near_pairs) for part in near_own]
    far_acc, near_acc = own_rest(far_own, near_own, match, far_acc, near_acc)
    done = near_pair(near_own, near, near_acc, scale)
    far_acc, *outs = middle(far_own, far[:-1], far_acc, done)
    return last(far_own, far[-1], far_acc, scale, outs, LAST_TILE)


def solution(mesh):
    in_specs = (P("dp", None), P("dp", None), P("dp"), P())
    out_specs = (P("dp", None), P("dp", None))
    return jax.shard_map(local, mesh=mesh, in_specs=in_specs, out_specs=out_specs, check_vma=False)
```

```python
import functools
import math

import jax
import jax.numpy as jnp
from jax import lax
from jax.experimental import pallas as pl
from jax.experimental.pallas import tpu as pltpu
from jax.sharding import PartitionSpec as P

LOGIT_SCALE = 10.0
SCORE_OFFSET = -2.0
FAR_ROWS = (768, 256)
NEAR_ROWS = (512, 512)
OWN_TILE = 256
EVEN_HEAD = 1
ODD_HEAD = 2
LAST_TILE = 256
PICK_TILE = 128
PAIR_TILE = 512
NT = (((1,), (1,)), ((), ()))
NN = (((1,), (0,)), ((), ()))
TN = (((0,), (0,)), ((), ()))
VMEM = pl.BlockSpec(memory_space=pltpu.VMEM)
SMEM = pl.BlockSpec(memory_space=pltpu.SMEM)
ANY = pl.BlockSpec(memory_space=pl.ANY)


def mm(a, b, dims):
    return lax.dot_general(a, b, dims, preferred_element_type=jnp.float32)


def sigmoid(product):
    per_bit = 1.0 / math.log(2.0)
    return 1.0 / (1.0 + jnp.exp2(product * (-LOGIT_SCALE * per_bit) - SCORE_OFFSET * per_bit))


def in_vmem(x):
    return pltpu.with_memory_space_constraint(x, pltpu.VMEM)


def in_hbm(x):
    return pltpu.with_memory_space_constraint(x, pltpu.HBM)


def params(mib):
    return pltpu.CompilerParams(vmem_limit_bytes=mib << 20)


def cost(matmuls, rows, cols, depth):
    return pl.CostEstimate(flops=2 * matmuls * rows * cols * depth, bytes_accessed=0, transcendentals=0)


def is_even():
    return lax.rem(lax.axis_index("dp"), 2) == 0


def fetches(starts, images_ref, texts_ref, outs, sems):
    even = is_even()

    def copies(i, source):
        return [
            pltpu.make_async_copy(
                source.at[pl.ds(starts[i][0] + at, PICK_TILE), :], outs[i].at[pl.ds(at, PICK_TILE), :], sems.at[i, at // PICK_TILE]
            )
            for at in range(0, outs[i].shape[0], PICK_TILE)
        ]

    def begin(flipped):
        for i, (_, _, flip) in enumerate(starts):
            for copy in copies(i, images_ref if flip == flipped else texts_ref):
                copy.start()

    @pl.when(even)
    def _():
        begin(False)

    @pl.when(jnp.logical_not(even))
    def _():
        begin(True)

    def wait(i):
        for copy in copies(i, images_ref):
            copy.wait()

    return [functools.partial(wait, i) for i in range(len(starts))]


def semaphores(wanted):
    return pltpu.SemaphoreType.DMA((len(wanted), max(w[1] for w in wanted) // PICK_TILE))


def pick_kernel(wanted, images_ref, texts_ref, *refs):
    for wait in fetches(wanted, images_ref, texts_ref, refs[:-1], refs[-1]):
        wait()


def pick(images, texts, wanted):
    depth = images.shape[1]
    return pl.pallas_call(
        functools.partial(pick_kernel, wanted),
        out_shape=tuple(pltpu.VMEM((w[1], depth), images.dtype) for w in wanted),
        in_specs=[ANY] * 2,
        out_specs=(VMEM,) * len(wanted),
        scratch_shapes=[semaphores(wanted)],
        compiler_params=params(1),
    )(in_hbm(images), in_hbm(texts))


def across(coef, others):
    total, at = None, 0
    for other in others:
        part = mm(coef[:, at : at + other.shape[0]], other, NN)
        total = part if total is None else total + part
        at += other.shape[0]
    return total


def own_tiles(tiles, at, other_refs, match_ref, acc_a, acc_b):
    rows = acc_b.shape[0]
    even = is_even()
    first = lax.axis_index("dp") * rows
    match_row = match_ref[...] - first

    def load(t):
        ref, start = tiles[t]
        return ref[start : start + OWN_TILE, :]

    others = [ref[...] for ref in other_refs]

    def product_of(t):
        return jnp.concatenate([mm(load(t), other, NT) for other in others], axis=1)

    product = product_of(0)
    for t in range(len(tiles)):
        following = product_of(t + 1) if t + 1 < len(tiles) else None
        match_tile = jnp.broadcast_to(match_ref[:, at : at + OWN_TILE] - first, (128, OWN_TILE)).T
        match_col = jnp.concatenate([match_tile] * (rows // 128), axis=1)
        lane = lax.broadcasted_iota(jnp.int32, (OWN_TILE, rows), 1)
        row = lax.broadcasted_iota(jnp.int32, (OWN_TILE, rows), 0) + at
        gap = jnp.where(even, match_col - lane, match_row - row)
        coef = (sigmoid(product) - jnp.where(gap == 0, 1.0, 0.0)).astype(jnp.bfloat16)
        acc_a[at : at + OWN_TILE, :] = across(coef, others)
        term = mm(coef, load(t), TN)
        if at == 0:
            acc_b[...] = term
        else:
            acc_b[...] += term
        product = following
        at += OWN_TILE


def tiles_of(refs):
    return [(ref, start) for ref in refs for start in range(0, ref.shape[0], OWN_TILE)]


def head_kernel(wanted, bases, images_ref, texts_ref, match_ref, cotangent_ref, first_ref, *refs):
    *outs, acc_a, acc_b, scale_ref, sems = refs
    waits = fetches(wanted, images_ref, texts_ref, outs, sems)
    scale_ref[...] = jnp.full(scale_ref.shape, cotangent_ref[0] * (LOGIT_SCALE / acc_b.shape[0]), jnp.float32)
    tiles = tiles_of([first_ref])
    for wait in waits[:bases]:
        wait()
    own_tiles(tiles[:EVEN_HEAD], 0, outs[:bases], match_ref, acc_a, acc_b)

    @pl.when(jnp.logical_not(is_even()))
    def _():
        own_tiles(tiles[EVEN_HEAD:ODD_HEAD], EVEN_HEAD * OWN_TILE, outs[:bases], match_ref, acc_a, acc_b)

    for wait in waits[bases:]:
        wait()


def own_head(images, texts, match, cotangent, first, wanted, bases):
    rows, depth = images.shape
    return pl.pallas_call(
        functools.partial(head_kernel, wanted, bases),
        out_shape=(
            *(pltpu.VMEM((w[1], depth), images.dtype) for w in wanted),
            pltpu.VMEM((rows, depth), jnp.float32),
            pltpu.VMEM((rows, depth), jnp.float32),
            pltpu.VMEM((8, depth), jnp.float32),
        ),
        in_specs=[ANY, ANY, VMEM, SMEM, VMEM],
        out_specs=(VMEM,) * (len(wanted) + 3),
        scratch_shapes=[semaphores(wanted)],
        compiler_params=params(16),
        cost_estimate=cost(3, OWN_TILE * ODD_HEAD, rows, depth),
    )(in_hbm(images), in_hbm(texts), in_vmem(match), cotangent, in_vmem(first))


def rest_kernel(chunks, match_ref, *refs):
    a_refs, b_refs, (acc_a, acc_b) = refs[:chunks], refs[chunks:-4], refs[-2:]
    tiles = tiles_of(a_refs)[ODD_HEAD:]
    own_tiles(tiles, ODD_HEAD * OWN_TILE, b_refs, match_ref, acc_a, acc_b)


def own_rest(own, base, match, acc_a, acc_b):
    rows, depth = acc_a.shape
    n, given = len(own), 1 + len(own) + len(base)
    return pl.pallas_call(
        functools.partial(rest_kernel, n),
        out_shape=(pltpu.VMEM((rows, depth), jnp.float32), pltpu.VMEM((rows, depth), jnp.float32)),
        in_specs=[VMEM] * (given + 2),
        out_specs=(VMEM, VMEM),
        input_output_aliases={given: 0, given + 1: 1},
        compiler_params=params(16),
        cost_estimate=cost(3, rows - OWN_TILE * ODD_HEAD, rows, depth),
    )(in_vmem(match), *[in_vmem(o) for o in (*own, *base, acc_a, acc_b)])


def catch_up_kernel(match_ref, first_ref, later_ref, *refs):
    b_refs, (acc_a, acc_b) = refs[:-5], refs[-2:]
    tiles = tiles_of([first_ref])[EVEN_HEAD:ODD_HEAD]

    @pl.when(is_even())
    def _():
        own_tiles(tiles, EVEN_HEAD * OWN_TILE, b_refs, match_ref, acc_a, acc_b)


def catch_up(first, later, base, match, acc_a, acc_b):
    rows, depth = acc_a.shape
    given = 3 + len(base)
    return pl.pallas_call(
        catch_up_kernel,
        out_shape=(
            pltpu.VMEM(later.shape, later.dtype),
            pltpu.VMEM((rows, depth), jnp.float32),
            pltpu.VMEM((rows, depth), jnp.float32),
        ),
        in_specs=[VMEM] * (given + 2),
        out_specs=(VMEM,) * 3,
        input_output_aliases={2: 0, given: 1, given + 1: 2},
        compiler_params=params(16),
        cost_estimate=cost(3, OWN_TILE * (ODD_HEAD - EVEN_HEAD), rows, depth),
    )(in_vmem(match), *[in_vmem(o) for o in (first, later, *base, acc_a, acc_b)])


def pair_tiles(own_refs, other_refs, tile):
    tiles = [(ref, start) for ref in own_refs for start in range(0, ref.shape[0], tile)]
    sizes = [min(tile, ref.shape[0] - start) for ref, start in tiles]
    others = [ref[...] for ref in other_refs]

    def products(t):
        ref, start = tiles[t]
        own = ref[start : start + sizes[t], :]
        return [mm(own, other, NT) for other in others]

    at, held = 0, products(0)
    for t in range(len(tiles)):
        following = products(t + 1) if t + 1 < len(tiles) else None
        term = None
        for product, other in zip(held, others, strict=True):
            part = mm(sigmoid(product).astype(jnp.bfloat16), other, NN)
            term = part if term is None else term + part
        yield t, at, sizes[t], term
        at += sizes[t]
        held = following


def near_kernel(chunks, *refs):
    own_refs, other_refs, rest = refs[:chunks], refs[chunks : 2 * chunks], refs[2 * chunks :]
    acc_ref, scale_ref, wide_ref, narrow_ref = rest

    def go(out_ref):
        scale = scale_ref[0:1, :]
        for _, at, size, term in pair_tiles(own_refs, other_refs, PAIR_TILE):
            rows = pl.ds(at, size)
            out_ref[rows, :] = (scale * (acc_ref[rows, :] + term)).astype(out_ref.dtype)

    @pl.when(is_even())
    def _():
        go(wide_ref)

    @pl.when(jnp.logical_not(is_even()))
    def _():
        go(narrow_ref)


def near_pair(own, other, acc, scale):
    rows, depth = acc.shape
    n = len(own)
    return pl.pallas_call(
        functools.partial(near_kernel, n),
        out_shape=(pltpu.VMEM((rows, depth), jnp.float32), pltpu.VMEM((rows, depth), jnp.bfloat16)),
        in_specs=[VMEM] * (2 * n + 2),
        out_specs=(VMEM, VMEM),
        input_output_aliases={2 * n: 0},
        compiler_params=params(16),
        cost_estimate=cost(2, rows, rows, depth),
    )(*[in_vmem(o) for o in (*own, *other, acc, scale)])


def last_kernel(chunks, tile, *refs):
    own_refs, other_ref, acc_ref, scale_ref = refs[:chunks], *refs[chunks : chunks + 3]
    image_ref, text_ref, wide, narrow, sems = refs[-5:]

    def go(stage, out_ref):
        scale = scale_ref[0:1, :]
        copies = []
        for t, at, size, term in pair_tiles(own_refs, [other_ref], tile):
            rows = pl.ds(at, size)
            stage[rows, :] = (scale * (acc_ref[rows, :] + term)).astype(stage.dtype)
            copies.append(pltpu.make_async_copy(stage.at[rows, :], out_ref.at[rows, :], sems.at[t]))
            copies[-1].start()
        for copy in copies:
            copy.wait()

    @pl.when(is_even())
    def _():
        go(narrow, image_ref)

    @pl.when(jnp.logical_not(is_even()))
    def _():
        go(wide, text_ref)


def last(own, other, acc, scale, outs, tile):
    rows, depth = acc.shape
    n = len(own)
    return pl.pallas_call(
        functools.partial(last_kernel, n, tile),
        out_shape=(
            jax.ShapeDtypeStruct((rows, depth), jnp.bfloat16),
            jax.ShapeDtypeStruct((rows, depth), jnp.float32),
        ),
        in_specs=[VMEM] * (n + 3) + [ANY] * 2,
        out_specs=(ANY, ANY),
        scratch_shapes=[
            pltpu.VMEM((rows, depth), jnp.float32),
            pltpu.VMEM((rows, depth), jnp.bfloat16),
            pltpu.SemaphoreType.DMA((rows // tile,)),
        ],
        input_output_aliases={n + 3 + i: i for i in range(2)},
        compiler_params=params(16),
        cost_estimate=cost(2, rows, other.shape[0], depth),
    )(*[in_vmem(o) for o in (*own, other, acc, scale)], *outs)


def middle_kernel(chunks, parts, *refs):
    own_refs, other_refs, rest = refs[:chunks], refs[chunks : chunks + parts], refs[chunks + parts :]
    acc_ref, wide_ref, narrow_ref, out_ref, image_ref, text_ref, sems = rest
    tile = acc_ref.shape[0] // sems.shape[0]

    def move(source, target, act):
        for i in range(sems.shape[0]):
            rows = pl.ds(i * tile, tile)
            act(pltpu.make_async_copy(source.at[rows, :], target.at[rows, :], sems.at[i]))

    def moves(act):
        @pl.when(is_even())
        def _():
            move(wide_ref, text_ref, act)

        @pl.when(jnp.logical_not(is_even()))
        def _():
            move(narrow_ref, image_ref, act)

    moves(lambda copy: copy.start())
    for _, at, size, term in pair_tiles(own_refs, other_refs, PAIR_TILE):
        rows = pl.ds(at, size)
        out_ref[rows, :] = acc_ref[rows, :] + term
    moves(lambda copy: copy.wait())


def middle(own, other, acc, done):
    rows, depth = acc.shape
    n, parts = len(own), len(other)
    return pl.pallas_call(
        functools.partial(middle_kernel, n, parts),
        out_shape=(
            pltpu.VMEM((rows, depth), jnp.float32),
            jax.ShapeDtypeStruct((rows, depth), jnp.bfloat16),
            jax.ShapeDtypeStruct((rows, depth), jnp.float32),
        ),
        in_specs=[VMEM] * (n + parts + 3),
        out_specs=(VMEM, ANY, ANY),
        scratch_shapes=[pltpu.SemaphoreType.DMA((4,))],
        input_output_aliases={n + parts: 0},
        compiler_params=params(16),
        cost_estimate=cost(2, rows, sum(o.shape[0] for o in other), depth),
    )(*[in_vmem(o) for o in (*own, *other, acc, *done)])


def spans(counts, flip):
    start = 0
    for count in counts:
        yield start, count, flip
        start += count


def local(images, texts, positive, loss_cotangent):
    rows = images.shape[0]
    size = lax.axis_size("dp")
    far_pairs = [(p, (p - 1) % size if p % 2 == 0 else (p + 1) % size) for p in range(size)]
    near_pairs = [(p, p + 1 if p % 2 == 0 else p - 1) for p in range(size)]
    match = positive.reshape(1, rows)
    (first,) = pick(images, texts, list(spans(FAR_ROWS, False))[:1])
    wanted = list(spans(NEAR_ROWS, True)) + list(spans(FAR_ROWS, False))[1:]
    bases = len(NEAR_ROWS)
    cotangent, first = lax.optimization_barrier((loss_cotangent, first))
    *picked, far_acc, near_acc, scale = own_head(images, texts, match, cotangent.reshape(1), first, wanted, bases)
    near_own = picked[:bases]
    later, far_acc, near_acc = catch_up(first, picked[bases], near_own, match, far_acc, near_acc)
    far_own = [first, later]
    far = [lax.ppermute(part, "dp", far_pairs) for part in far_own]
    near = [lax.ppermute(part, "dp", near_pairs) for part in near_own]
    far_acc, near_acc = own_rest(far_own, near_own, match, far_acc, near_acc)
    done = near_pair(near_own, near, near_acc, scale)
    far_acc, *outs = middle(far_own, far[:-1], far_acc, done)
    return last(far_own, far[-1], far_acc, scale, outs, LAST_TILE)


def solution(mesh):
    in_specs = (P("dp", None), P("dp", None), P("dp"), P())
    out_specs = (P("dp", None), P("dp", None))
    return jax.shard_map(local, mesh=mesh, in_specs=in_specs, out_specs=out_specs, check_vma=False)
```

```python
import functools
import math

import jax
import jax.numpy as jnp
from jax import lax
from jax.experimental import pallas as pl
from jax.experimental.pallas import tpu as pltpu
from jax.sharding import PartitionSpec as P

LOGIT_SCALE = 10.0
SCORE_OFFSET = -2.0
FAR_ROWS = (768, 256)
NEAR_ROWS = (512, 512)
OWN_TILE = 256
EVEN_HEAD = 1
ODD_HEAD = 2
LAST_TILE = 256
PICK_TILE = 128
PAIR_TILE = 512
NT = (((1,), (1,)), ((), ()))
NN = (((1,), (0,)), ((), ()))
TN = (((0,), (0,)), ((), ()))
VMEM = pl.BlockSpec(memory_space=pltpu.VMEM)
SMEM = pl.BlockSpec(memory_space=pltpu.SMEM)
ANY = pl.BlockSpec(memory_space=pl.ANY)


def mm(a, b, dims):
    return lax.dot_general(a, b, dims, preferred_element_type=jnp.float32)


def sigmoid(product):
    per_bit = 1.0 / math.log(2.0)
    return 1.0 / (1.0 + jnp.exp2(product * (-LOGIT_SCALE * per_bit) - SCORE_OFFSET * per_bit))


def in_vmem(x):
    return pltpu.with_memory_space_constraint(x, pltpu.VMEM)


def in_hbm(x):
    return pltpu.with_memory_space_constraint(x, pltpu.HBM)


def params(mib):
    return pltpu.CompilerParams(vmem_limit_bytes=mib << 20)


def cost(matmuls, rows, cols, depth):
    return pl.CostEstimate(flops=2 * matmuls * rows * cols * depth, bytes_accessed=0, transcendentals=0)


def is_even():
    return lax.rem(lax.axis_index("dp"), 2) == 0


def fetches(starts, images_ref, texts_ref, outs, sems):
    even = is_even()

    def copies(i, source):
        return [
            pltpu.make_async_copy(
                source.at[pl.ds(starts[i][0] + at, PICK_TILE), :], outs[i].at[pl.ds(at, PICK_TILE), :], sems.at[i, at // PICK_TILE]
            )
            for at in range(0, outs[i].shape[0], PICK_TILE)
        ]

    def begin(flipped):
        for i, (_, _, flip) in enumerate(starts):
            for copy in copies(i, images_ref if flip == flipped else texts_ref):
                copy.start()

    @pl.when(even)
    def _():
        begin(False)

    @pl.when(jnp.logical_not(even))
    def _():
        begin(True)

    def wait(i):
        for copy in copies(i, images_ref):
            copy.wait()

    return [functools.partial(wait, i) for i in range(len(starts))]


def semaphores(wanted):
    return pltpu.SemaphoreType.DMA((len(wanted), max(w[1] for w in wanted) // PICK_TILE))


def pick_kernel(wanted, images_ref, texts_ref, *refs):
    for wait in fetches(wanted, images_ref, texts_ref, refs[:-1], refs[-1]):
        wait()


def pick(images, texts, wanted):
    depth = images.shape[1]
    return pl.pallas_call(
        functools.partial(pick_kernel, wanted),
        out_shape=tuple(pltpu.VMEM((w[1], depth), images.dtype) for w in wanted),
        in_specs=[ANY] * 2,
        out_specs=(VMEM,) * len(wanted),
        scratch_shapes=[semaphores(wanted)],
        compiler_params=params(1),
    )(in_hbm(images), in_hbm(texts))


def across(coef, others):
    total, at = None, 0
    for other in others:
        part = mm(coef[:, at : at + other.shape[0]], other, NN)
        total = part if total is None else total + part
        at += other.shape[0]
    return total


def own_tiles(tiles, at, other_refs, match_ref, acc_a, acc_b):
    rows = acc_b.shape[0]
    even = is_even()
    first = lax.axis_index("dp") * rows
    match_row = match_ref[...] - first

    def load(t):
        ref, start = tiles[t]
        return ref[start : start + OWN_TILE, :]

    others = [ref[...] for ref in other_refs]

    def product_of(t):
        return jnp.concatenate([mm(load(t), other, NT) for other in others], axis=1)

    product = product_of(0)
    for t in range(len(tiles)):
        following = product_of(t + 1) if t + 1 < len(tiles) else None
        match_tile = jnp.broadcast_to(match_ref[:, at : at + OWN_TILE] - first, (128, OWN_TILE)).T
        match_col = jnp.concatenate([match_tile] * (rows // 128), axis=1)
        lane = lax.broadcasted_iota(jnp.int32, (OWN_TILE, rows), 1)
        row = lax.broadcasted_iota(jnp.int32, (OWN_TILE, rows), 0) + at
        gap = jnp.where(even, match_col - lane, match_row - row)
        coef = (sigmoid(product) - jnp.where(gap == 0, 1.0, 0.0)).astype(jnp.bfloat16)
        acc_a[at : at + OWN_TILE, :] = across(coef, others)
        term = mm(coef, load(t), TN)
        if at == 0:
            acc_b[...] = term
        else:
            acc_b[...] += term
        product = following
        at += OWN_TILE


def tiles_of(refs):
    return [(ref, start) for ref in refs for start in range(0, ref.shape[0], OWN_TILE)]


def head_kernel(wanted, bases, images_ref, texts_ref, match_ref, cotangent_ref, first_ref, *refs):
    *outs, acc_a, acc_b, scale_ref, sems = refs
    waits = fetches(wanted, images_ref, texts_ref, outs, sems)
    scale_ref[...] = jnp.full(scale_ref.shape, cotangent_ref[0] * (LOGIT_SCALE / acc_b.shape[0]), jnp.float32)
    tiles = tiles_of([first_ref])
    for wait in waits[:bases]:
        wait()
    own_tiles(tiles[:EVEN_HEAD], 0, outs[:bases], match_ref, acc_a, acc_b)

    @pl.when(jnp.logical_not(is_even()))
    def _():
        own_tiles(tiles[EVEN_HEAD:ODD_HEAD], EVEN_HEAD * OWN_TILE, outs[:bases], match_ref, acc_a, acc_b)

    for wait in waits[bases:]:
        wait()


def own_head(images, texts, match, cotangent, first, wanted, bases):
    rows, depth = images.shape
    return pl.pallas_call(
        functools.partial(head_kernel, wanted, bases),
        out_shape=(
            *(pltpu.VMEM((w[1], depth), images.dtype) for w in wanted),
            pltpu.VMEM((rows, depth), jnp.float32),
            pltpu.VMEM((rows, depth), jnp.float32),
            pltpu.VMEM((8, depth), jnp.float32),
        ),
        in_specs=[ANY, ANY, VMEM, SMEM, VMEM],
        out_specs=(VMEM,) * (len(wanted) + 3),
        scratch_shapes=[semaphores(wanted)],
        compiler_params=params(16),
        cost_estimate=cost(3, OWN_TILE * ODD_HEAD, rows, depth),
    )(in_hbm(images), in_hbm(texts), in_vmem(match), cotangent, in_vmem(first))


def rest_kernel(chunks, match_ref, *refs):
    a_refs, b_refs, (acc_a, acc_b) = refs[:chunks], refs[chunks:-4], refs[-2:]
    tiles = tiles_of(a_refs)[ODD_HEAD:]
    own_tiles(tiles, ODD_HEAD * OWN_TILE, b_refs, match_ref, acc_a, acc_b)


def own_rest(own, base, match, acc_a, acc_b):
    rows, depth = acc_a.shape
    n, given = len(own), 1 + len(own) + len(base)
    return pl.pallas_call(
        functools.partial(rest_kernel, n),
        out_shape=(pltpu.VMEM((rows, depth), jnp.float32), pltpu.VMEM((rows, depth), jnp.float32)),
        in_specs=[VMEM] * (given + 2),
        out_specs=(VMEM, VMEM),
        input_output_aliases={given: 0, given + 1: 1},
        compiler_params=params(16),
        cost_estimate=cost(3, rows - OWN_TILE * ODD_HEAD, rows, depth),
    )(in_vmem(match), *[in_vmem(o) for o in (*own, *base, acc_a, acc_b)])


def catch_up_kernel(match_ref, first_ref, later_ref, *refs):
    b_refs, (acc_a, acc_b) = refs[:-5], refs[-2:]
    tiles = tiles_of([first_ref])[EVEN_HEAD:ODD_HEAD]

    @pl.when(is_even())
    def _():
        own_tiles(tiles, EVEN_HEAD * OWN_TILE, b_refs, match_ref, acc_a, acc_b)


def catch_up(first, later, base, match, acc_a, acc_b):
    rows, depth = acc_a.shape
    given = 3 + len(base)
    return pl.pallas_call(
        catch_up_kernel,
        out_shape=(
            pltpu.VMEM(later.shape, later.dtype),
            pltpu.VMEM((rows, depth), jnp.float32),
            pltpu.VMEM((rows, depth), jnp.float32),
        ),
        in_specs=[VMEM] * (given + 2),
        out_specs=(VMEM,) * 3,
        input_output_aliases={2: 0, given: 1, given + 1: 2},
        compiler_params=params(16),
        cost_estimate=cost(3, OWN_TILE * (ODD_HEAD - EVEN_HEAD), rows, depth),
    )(in_vmem(match), *[in_vmem(o) for o in (first, later, *base, acc_a, acc_b)])


def pair_tiles(own_refs, other_refs, tile):
    tiles = [(ref, start) for ref in own_refs for start in range(0, ref.shape[0], tile)]
    sizes = [min(tile, ref.shape[0] - start) for ref, start in tiles]
    others = [ref[...] for ref in other_refs]

    def products(t):
        ref, start = tiles[t]
        own = ref[start : start + sizes[t], :]
        return [mm(own, other, NT) for other in others]

    at, held = 0, products(0)
    for t in range(len(tiles)):
        following = products(t + 1) if t + 1 < len(tiles) else None
        term = None
        for product, other in zip(held, others, strict=True):
            part = mm(sigmoid(product).astype(jnp.bfloat16), other, NN)
            term = part if term is None else term + part
        yield t, at, sizes[t], term
        at += sizes[t]
        held = following


def near_kernel(chunks, *refs):
    own_refs, other_refs, rest = refs[:chunks], refs[chunks : 2 * chunks], refs[2 * chunks :]
    acc_ref, scale_ref, wide_ref, narrow_ref = rest

    def go(out_ref):
        scale = scale_ref[0:1, :]
        for _, at, size, term in pair_tiles(own_refs, other_refs, PAIR_TILE):
            rows = pl.ds(at, size)
            out_ref[rows, :] = (scale * (acc_ref[rows, :] + term)).astype(out_ref.dtype)

    @pl.when(is_even())
    def _():
        go(wide_ref)

    @pl.when(jnp.logical_not(is_even()))
    def _():
        go(narrow_ref)


def near_pair(own, other, acc, scale):
    rows, depth = acc.shape
    n = len(own)
    return pl.pallas_call(
        functools.partial(near_kernel, n),
        out_shape=(pltpu.VMEM((rows, depth), jnp.float32), pltpu.VMEM((rows, depth), jnp.bfloat16)),
        in_specs=[VMEM] * (2 * n + 2),
        out_specs=(VMEM, VMEM),
        compiler_params=params(16),
        cost_estimate=cost(2, rows, rows, depth),
    )(*[in_vmem(o) for o in (*own, *other, acc, scale)])


def last_kernel(chunks, tile, *refs):
    own_refs, other_ref, acc_ref, scale_ref = refs[:chunks], *refs[chunks : chunks + 3]
    image_ref, text_ref, wide, narrow, sems = refs[-5:]

    def go(stage, out_ref):
        scale = scale_ref[0:1, :]
        copies = []
        for t, at, size, term in pair_tiles(own_refs, [other_ref], tile):
            rows = pl.ds(at, size)
            stage[rows, :] = (scale * (acc_ref[rows, :] + term)).astype(stage.dtype)
            copies.append(pltpu.make_async_copy(stage.at[rows, :], out_ref.at[rows, :], sems.at[t]))
            copies[-1].start()
        for copy in copies:
            copy.wait()

    @pl.when(is_even())
    def _():
        go(narrow, image_ref)

    @pl.when(jnp.logical_not(is_even()))
    def _():
        go(wide, text_ref)


def last(own, other, acc, scale, outs, tile):
    rows, depth = acc.shape
    n = len(own)
    return pl.pallas_call(
        functools.partial(last_kernel, n, tile),
        out_shape=(
            jax.ShapeDtypeStruct((rows, depth), jnp.bfloat16),
            jax.ShapeDtypeStruct((rows, depth), jnp.float32),
        ),
        in_specs=[VMEM] * (n + 3) + [ANY] * 2,
        out_specs=(ANY, ANY),
        scratch_shapes=[
            pltpu.VMEM((rows, depth), jnp.float32),
            pltpu.VMEM((rows, depth), jnp.bfloat16),
            pltpu.SemaphoreType.DMA((rows // tile,)),
        ],
        input_output_aliases={n + 3 + i: i for i in range(2)},
        compiler_params=params(16),
        cost_estimate=cost(2, rows, other.shape[0], depth),
    )(*[in_vmem(o) for o in (*own, other, acc, scale)], *outs)


def middle_kernel(chunks, parts, *refs):
    own_refs, other_refs, rest = refs[:chunks], refs[chunks : chunks + parts], refs[chunks + parts :]
    acc_ref, wide_ref, narrow_ref, out_ref, image_ref, text_ref, sems = rest
    tile = acc_ref.shape[0] // sems.shape[0]

    def move(source, target, act):
        for i in range(sems.shape[0]):
            rows = pl.ds(i * tile, tile)
            act(pltpu.make_async_copy(source.at[rows, :], target.at[rows, :], sems.at[i]))

    def moves(act):
        @pl.when(is_even())
        def _():
            move(wide_ref, text_ref, act)

        @pl.when(jnp.logical_not(is_even()))
        def _():
            move(narrow_ref, image_ref, act)

    moves(lambda copy: copy.start())
    for _, at, size, term in pair_tiles(own_refs, other_refs, PAIR_TILE):
        rows = pl.ds(at, size)
        out_ref[rows, :] = acc_ref[rows, :] + term
    moves(lambda copy: copy.wait())


def middle(own, other, acc, done):
    rows, depth = acc.shape
    n, parts = len(own), len(other)
    return pl.pallas_call(
        functools.partial(middle_kernel, n, parts),
        out_shape=(
            pltpu.VMEM((rows, depth), jnp.float32),
            jax.ShapeDtypeStruct((rows, depth), jnp.bfloat16),
            jax.ShapeDtypeStruct((rows, depth), jnp.float32),
        ),
        in_specs=[VMEM] * (n + parts + 3),
        out_specs=(VMEM, ANY, ANY),
        scratch_shapes=[pltpu.SemaphoreType.DMA((4,))],
        input_output_aliases={n + parts: 0},
        compiler_params=params(16),
        cost_estimate=cost(2, rows, sum(o.shape[0] for o in other), depth),
    )(*[in_vmem(o) for o in (*own, *other, acc, *done)])


def spans(counts, flip):
    start = 0
    for count in counts:
        yield start, count, flip
        start += count


def local(images, texts, positive, loss_cotangent):
    rows = images.shape[0]
    size = lax.axis_size("dp")
    far_pairs = [(p, (p - 1) % size if p % 2 == 0 else (p + 1) % size) for p in range(size)]
    near_pairs = [(p, p + 1 if p % 2 == 0 else p - 1) for p in range(size)]
    match = positive.reshape(1, rows)
    (first,) = pick(images, texts, list(spans(FAR_ROWS, False))[:1])
    wanted = list(spans(NEAR_ROWS, True)) + list(spans(FAR_ROWS, False))[1:]
    bases = len(NEAR_ROWS)
    cotangent, first = lax.optimization_barrier((loss_cotangent, first))
    *picked, far_acc, near_acc, scale = own_head(images, texts, match, cotangent.reshape(1), first, wanted, bases)
    near_own = picked[:bases]
    later, far_acc, near_acc = catch_up(first, picked[bases], near_own, match, far_acc, near_acc)
    far_own = [first, later]
    far = [lax.ppermute(part, "dp", far_pairs) for part in far_own]
    near = [lax.ppermute(part, "dp", near_pairs) for part in near_own]
    far_acc, near_acc = own_rest(far_own, near_own, match, far_acc, near_acc)
    done = near_pair(near_own, near, near_acc, scale)
    far_acc, *outs = middle(far_own, far[:-1], far_acc, done)
    return last(far_own, far[-1], far_acc, scale, outs, LAST_TILE)


def solution(mesh):
    in_specs = (P("dp", None), P("dp", None), P("dp"), P())
    out_specs = (P("dp", None), P("dp", None))
    return jax.shard_map(local, mesh=mesh, in_specs=in_specs, out_specs=out_specs, check_vma=False)
```

```python
import functools
import math

import jax
import jax.numpy as jnp
from jax import lax
from jax.experimental import pallas as pl
from jax.experimental.pallas import tpu as pltpu
from jax.sharding import PartitionSpec as P

LOGIT_SCALE = 10.0
SCORE_OFFSET = -2.0
FAR_ROWS = (768, 256)
NEAR_ROWS = (512, 512)
OWN_TILE = 256
EVEN_HEAD = 1
ODD_HEAD = 2
LAST_TILE = 256
PICK_TILE = 256
PAIR_TILE = 512
NT = (((1,), (1,)), ((), ()))
NN = (((1,), (0,)), ((), ()))
TN = (((0,), (0,)), ((), ()))
VMEM = pl.BlockSpec(memory_space=pltpu.VMEM)
SMEM = pl.BlockSpec(memory_space=pltpu.SMEM)
ANY = pl.BlockSpec(memory_space=pl.ANY)


def mm(a, b, dims):
    return lax.dot_general(a, b, dims, preferred_element_type=jnp.float32)


def sigmoid(product):
    per_bit = 1.0 / math.log(2.0)
    return 1.0 / (1.0 + jnp.exp2(product * (-LOGIT_SCALE * per_bit) - SCORE_OFFSET * per_bit))


def in_vmem(x):
    return pltpu.with_memory_space_constraint(x, pltpu.VMEM)


def in_hbm(x):
    return pltpu.with_memory_space_constraint(x, pltpu.HBM)


def params(mib):
    return pltpu.CompilerParams(vmem_limit_bytes=mib << 20)


def cost(matmuls, rows, cols, depth):
    return pl.CostEstimate(flops=2 * matmuls * rows * cols * depth, bytes_accessed=0, transcendentals=0)


def is_even():
    return lax.rem(lax.axis_index("dp"), 2) == 0


def fetches(starts, images_ref, texts_ref, outs, sems):
    even = is_even()

    def copies(i, source):
        return [
            pltpu.make_async_copy(
                source.at[pl.ds(starts[i][0] + at, PICK_TILE), :], outs[i].at[pl.ds(at, PICK_TILE), :], sems.at[i, at // PICK_TILE]
            )
            for at in range(0, outs[i].shape[0], PICK_TILE)
        ]

    def begin(flipped):
        for i, (_, _, flip) in enumerate(starts):
            for copy in copies(i, images_ref if flip == flipped else texts_ref):
                copy.start()

    @pl.when(even)
    def _():
        begin(False)

    @pl.when(jnp.logical_not(even))
    def _():
        begin(True)

    def wait(i):
        for copy in copies(i, images_ref):
            copy.wait()

    return [functools.partial(wait, i) for i in range(len(starts))]


def semaphores(wanted):
    return pltpu.SemaphoreType.DMA((len(wanted), max(w[1] for w in wanted) // PICK_TILE))


def pick_kernel(wanted, images_ref, texts_ref, *refs):
    for wait in fetches(wanted, images_ref, texts_ref, refs[:-1], refs[-1]):
        wait()


def pick(images, texts, wanted):
    depth = images.shape[1]
    return pl.pallas_call(
        functools.partial(pick_kernel, wanted),
        out_shape=tuple(pltpu.VMEM((w[1], depth), images.dtype) for w in wanted),
        in_specs=[ANY] * 2,
        out_specs=(VMEM,) * len(wanted),
        scratch_shapes=[semaphores(wanted)],
        compiler_params=params(1),
    )(in_hbm(images), in_hbm(texts))


def across(coef, others):
    total, at = None, 0
    for other in others:
        part = mm(coef[:, at : at + other.shape[0]], other, NN)
        total = part if total is None else total + part
        at += other.shape[0]
    return total


def own_tiles(tiles, at, other_refs, match_ref, acc_a, acc_b):
    rows = acc_b.shape[0]
    even = is_even()
    first = lax.axis_index("dp") * rows
    match_row = match_ref[...] - first

    def load(t):
        ref, start = tiles[t]
        return ref[start : start + OWN_TILE, :]

    others = [ref[...] for ref in other_refs]

    def product_of(t):
        return jnp.concatenate([mm(load(t), other, NT) for other in others], axis=1)

    product = product_of(0)
    for t in range(len(tiles)):
        following = product_of(t + 1) if t + 1 < len(tiles) else None
        match_tile = jnp.broadcast_to(match_ref[:, at : at + OWN_TILE] - first, (128, OWN_TILE)).T
        match_col = jnp.concatenate([match_tile] * (rows // 128), axis=1)
        lane = lax.broadcasted_iota(jnp.int32, (OWN_TILE, rows), 1)
        row = lax.broadcasted_iota(jnp.int32, (OWN_TILE, rows), 0) + at
        gap = jnp.where(even, match_col - lane, match_row - row)
        coef = (sigmoid(product) - jnp.where(gap == 0, 1.0, 0.0)).astype(jnp.bfloat16)
        acc_a[at : at + OWN_TILE, :] = across(coef, others)
        term = mm(coef, load(t), TN)
        if at == 0:
            acc_b[...] = term
        else:
            acc_b[...] += term
        product = following
        at += OWN_TILE


def tiles_of(refs):
    return [(ref, start) for ref in refs for start in range(0, ref.shape[0], OWN_TILE)]


def head_kernel(wanted, bases, images_ref, texts_ref, match_ref, cotangent_ref, first_ref, *refs):
    *outs, acc_a, acc_b, scale_ref, sems = refs
    waits = fetches(wanted, images_ref, texts_ref, outs, sems)
    scale_ref[...] = jnp.full(scale_ref.shape, cotangent_ref[0] * (LOGIT_SCALE / acc_b.shape[0]), jnp.float32)
    tiles = tiles_of([first_ref])
    for wait in waits[:bases]:
        wait()
    own_tiles(tiles[:EVEN_HEAD], 0, outs[:bases], match_ref, acc_a, acc_b)

    @pl.when(jnp.logical_not(is_even()))
    def _():
        own_tiles(tiles[EVEN_HEAD:ODD_HEAD], EVEN_HEAD * OWN_TILE, outs[:bases], match_ref, acc_a, acc_b)

    for wait in waits[bases:]:
        wait()


def own_head(images, texts, match, cotangent, first, wanted, bases):
    rows, depth = images.shape
    return pl.pallas_call(
        functools.partial(head_kernel, wanted, bases),
        out_shape=(
            *(pltpu.VMEM((w[1], depth), images.dtype) for w in wanted),
            pltpu.VMEM((rows, depth), jnp.float32),
            pltpu.VMEM((rows, depth), jnp.float32),
            pltpu.VMEM((8, depth), jnp.float32),
        ),
        in_specs=[ANY, ANY, VMEM, SMEM, VMEM],
        out_specs=(VMEM,) * (len(wanted) + 3),
        scratch_shapes=[semaphores(wanted)],
        compiler_params=params(16),
        cost_estimate=cost(3, OWN_TILE * ODD_HEAD, rows, depth),
    )(in_hbm(images), in_hbm(texts), in_vmem(match), cotangent, in_vmem(first))


def rest_kernel(chunks, match_ref, *refs):
    a_refs, b_refs, (acc_a, acc_b) = refs[:chunks], refs[chunks:-4], refs[-2:]
    tiles = tiles_of(a_refs)[ODD_HEAD:]
    own_tiles(tiles, ODD_HEAD * OWN_TILE, b_refs, match_ref, acc_a, acc_b)


def own_rest(own, base, match, acc_a, acc_b):
    rows, depth = acc_a.shape
    n, given = len(own), 1 + len(own) + len(base)
    return pl.pallas_call(
        functools.partial(rest_kernel, n),
        out_shape=(pltpu.VMEM((rows, depth), jnp.float32), pltpu.VMEM((rows, depth), jnp.float32)),
        in_specs=[VMEM] * (given + 2),
        out_specs=(VMEM, VMEM),
        input_output_aliases={given: 0, given + 1: 1},
        compiler_params=params(16),
        cost_estimate=cost(3, rows - OWN_TILE * ODD_HEAD, rows, depth),
    )(in_vmem(match), *[in_vmem(o) for o in (*own, *base, acc_a, acc_b)])


def catch_up_kernel(match_ref, first_ref, later_ref, *refs):
    b_refs, (acc_a, acc_b) = refs[:-5], refs[-2:]
    tiles = tiles_of([first_ref])[EVEN_HEAD:ODD_HEAD]

    @pl.when(is_even())
    def _():
        own_tiles(tiles, EVEN_HEAD * OWN_TILE, b_refs, match_ref, acc_a, acc_b)


def catch_up(first, later, base, match, acc_a, acc_b):
    rows, depth = acc_a.shape
    given = 3 + len(base)
    return pl.pallas_call(
        catch_up_kernel,
        out_shape=(
            pltpu.VMEM(later.shape, later.dtype),
            pltpu.VMEM((rows, depth), jnp.float32),
            pltpu.VMEM((rows, depth), jnp.float32),
        ),
        in_specs=[VMEM] * (given + 2),
        out_specs=(VMEM,) * 3,
        input_output_aliases={2: 0, given: 1, given + 1: 2},
        compiler_params=params(16),
        cost_estimate=cost(3, OWN_TILE * (ODD_HEAD - EVEN_HEAD), rows, depth),
    )(in_vmem(match), *[in_vmem(o) for o in (first, later, *base, acc_a, acc_b)])


def pair_tiles(own_refs, other_refs, tile):
    tiles = [(ref, start) for ref in own_refs for start in range(0, ref.shape[0], tile)]
    sizes = [min(tile, ref.shape[0] - start) for ref, start in tiles]
    others = [ref[...] for ref in other_refs]

    def products(t):
        ref, start = tiles[t]
        own = ref[start : start + sizes[t], :]
        return [mm(own, other, NT) for other in others]

    at, held = 0, products(0)
    for t in range(len(tiles)):
        following = products(t + 1) if t + 1 < len(tiles) else None
        term = None
        for product, other in zip(held, others, strict=True):
            part = mm(sigmoid(product).astype(jnp.bfloat16), other, NN)
            term = part if term is None else term + part
        yield t, at, sizes[t], term
        at += sizes[t]
        held = following


def near_kernel(chunks, *refs):
    own_refs, other_refs, rest = refs[:chunks], refs[chunks : 2 * chunks], refs[2 * chunks :]
    acc_ref, scale_ref, wide_ref, narrow_ref = rest

    def go(out_ref):
        scale = scale_ref[0:1, :]
        for _, at, size, term in pair_tiles(own_refs, other_refs, PAIR_TILE):
            rows = pl.ds(at, size)
            out_ref[rows, :] = (scale * (acc_ref[rows, :] + term)).astype(out_ref.dtype)

    @pl.when(is_even())
    def _():
        go(wide_ref)

    @pl.when(jnp.logical_not(is_even()))
    def _():
        go(narrow_ref)


def near_pair(own, other, acc, scale):
    rows, depth = acc.shape
    n = len(own)
    return pl.pallas_call(
        functools.partial(near_kernel, n),
        out_shape=(pltpu.VMEM((rows, depth), jnp.float32), pltpu.VMEM((rows, depth), jnp.bfloat16)),
        in_specs=[VMEM] * (2 * n + 2),
        out_specs=(VMEM, VMEM),
        compiler_params=params(16),
        cost_estimate=cost(2, rows, rows, depth),
    )(*[in_vmem(o) for o in (*own, *other, acc, scale)])


def last_kernel(chunks, tile, *refs):
    own_refs, other_ref, acc_ref, scale_ref = refs[:chunks], *refs[chunks : chunks + 3]
    image_ref, text_ref, wide, narrow, sems = refs[-5:]

    def go(stage, out_ref):
        scale = scale_ref[0:1, :]
        copies = []
        for t, at, size, term in pair_tiles(own_refs, [other_ref], tile):
            rows = pl.ds(at, size)
            stage[rows, :] = (scale * (acc_ref[rows, :] + term)).astype(stage.dtype)
            copies.append(pltpu.make_async_copy(stage.at[rows, :], out_ref.at[rows, :], sems.at[t]))
            copies[-1].start()
        for copy in copies:
            copy.wait()

    @pl.when(is_even())
    def _():
        go(narrow, image_ref)

    @pl.when(jnp.logical_not(is_even()))
    def _():
        go(wide, text_ref)


def last(own, other, acc, scale, outs, tile):
    rows, depth = acc.shape
    n = len(own)
    return pl.pallas_call(
        functools.partial(last_kernel, n, tile),
        out_shape=(
            jax.ShapeDtypeStruct((rows, depth), jnp.bfloat16),
            jax.ShapeDtypeStruct((rows, depth), jnp.float32),
        ),
        in_specs=[VMEM] * (n + 3) + [ANY] * 2,
        out_specs=(ANY, ANY),
        scratch_shapes=[
            pltpu.VMEM((rows, depth), jnp.float32),
            pltpu.VMEM((rows, depth), jnp.bfloat16),
            pltpu.SemaphoreType.DMA((rows // tile,)),
        ],
        input_output_aliases={n + 3 + i: i for i in range(2)},
        compiler_params=params(16),
        cost_estimate=cost(2, rows, other.shape[0], depth),
    )(*[in_vmem(o) for o in (*own, other, acc, scale)], *outs)


def middle_kernel(chunks, parts, *refs):
    own_refs, other_refs, rest = refs[:chunks], refs[chunks : chunks + parts], refs[chunks + parts :]
    acc_ref, wide_ref, narrow_ref, out_ref, image_ref, text_ref, sems = rest
    tile = acc_ref.shape[0] // sems.shape[0]

    def move(source, target, act):
        for i in range(sems.shape[0]):
            rows = pl.ds(i * tile, tile)
            act(pltpu.make_async_copy(source.at[rows, :], target.at[rows, :], sems.at[i]))

    def moves(act):
        @pl.when(is_even())
        def _():
            move(wide_ref, text_ref, act)

        @pl.when(jnp.logical_not(is_even()))
        def _():
            move(narrow_ref, image_ref, act)

    moves(lambda copy: copy.start())
    for _, at, size, term in pair_tiles(own_refs, other_refs, PAIR_TILE):
        rows = pl.ds(at, size)
        out_ref[rows, :] = acc_ref[rows, :] + term
    moves(lambda copy: copy.wait())


def middle(own, other, acc, done):
    rows, depth = acc.shape
    n, parts = len(own), len(other)
    return pl.pallas_call(
        functools.partial(middle_kernel, n, parts),
        out_shape=(
            pltpu.VMEM((rows, depth), jnp.float32),
            jax.ShapeDtypeStruct((rows, depth), jnp.bfloat16),
            jax.ShapeDtypeStruct((rows, depth), jnp.float32),
        ),
        in_specs=[VMEM] * (n + parts + 3),
        out_specs=(VMEM, ANY, ANY),
        scratch_shapes=[pltpu.SemaphoreType.DMA((4,))],

        compiler_params=params(16),
        cost_estimate=cost(2, rows, sum(o.shape[0] for o in other), depth),
    )(*[in_vmem(o) for o in (*own, *other, acc, *done)])


def spans(counts, flip):
    start = 0
    for count in counts:
        yield start, count, flip
        start += count


def local(images, texts, positive, loss_cotangent):
    rows = images.shape[0]
    size = lax.axis_size("dp")
    far_pairs = [(p, (p - 1) % size if p % 2 == 0 else (p + 1) % size) for p in range(size)]
    near_pairs = [(p, p + 1 if p % 2 == 0 else p - 1) for p in range(size)]
    match = positive.reshape(1, rows)
    (first,) = pick(images, texts, list(spans(FAR_ROWS, False))[:1])
    wanted = list(spans(NEAR_ROWS, True)) + list(spans(FAR_ROWS, False))[1:]
    bases = len(NEAR_ROWS)
    cotangent, first = lax.optimization_barrier((loss_cotangent, first))
    *picked, far_acc, near_acc, scale = own_head(images, texts, match, cotangent.reshape(1), first, wanted, bases)
    near_own = picked[:bases]
    later, far_acc, near_acc = catch_up(first, picked[bases], near_own, match, far_acc, near_acc)
    far_own = [first, later]
    far = [lax.ppermute(part, "dp", far_pairs) for part in far_own]
    near = [lax.ppermute(part, "dp", near_pairs) for part in near_own]
    far_acc, near_acc = own_rest(far_own, near_own, match, far_acc, near_acc)
    done = near_pair(near_own, near, near_acc, scale)
    far_acc, *outs = middle(far_own, far[:-1], far_acc, done)
    return last(far_own, far[-1], far_acc, scale, outs, LAST_TILE)


def solution(mesh):
    in_specs = (P("dp", None), P("dp", None), P("dp"), P())
    out_specs = (P("dp", None), P("dp", None))
    return jax.shard_map(local, mesh=mesh, in_specs=in_specs, out_specs=out_specs, check_vma=False)
```
